256 devices in a mesh: fsdp: 32 (over x, z), group: 8 (over y, core).
Axes of the slice: x: 4, y: 4, z: 8, core: 2. Of those that a mesh axis runs over, the one named last changes fastest.
Arguments:
- grad: bfloat16 [4096, 28672], P(('fsdp', 'group')), may hold values from -6 to 6
- momentum: float32 [4096, 28672], P(('fsdp', 'group')), may hold values from -300 to 300
- second: float32 [4096, 28672], P(('fsdp', 'group')), may hold values from 0.2 to 5
- left_root: bfloat16 [192, 8, 8, 16, 1024], P('fsdp', None, 'group'), may hold values from -1 to 4
- right_root: bfloat16 [192, 8, 8, 16, 1024], P('fsdp', None, 'group'), may hold values from -1 to 4
- owner_table: int32 [112], replicated, may hold values from 0 to 31, as said below
Outputs:
- update: bfloat16 [4096, 28672], P(('fsdp', 'group'))
- new_momentum: float32 [4096, 28672], P(('fsdp', 'group'))
- new_second: float32 [4096, 28672], P(('fsdp', 'group'))
The draws below stay inside these ranges and needn't reach their ends.
Inputs may be any that keep to these rules, and one draw needn't show every extreme that they name: `owner_table`: each owner holds at most 6 blocks and some owner exactly 6; at most 2 blocks of one row block share an owner, and in some row block one owner has exactly 2.
All inputs are finite; a program needn't handle non-finite values.
Results may differ from the reference program's by a relative error of at most 0.025.
Values may be sent and summed in bfloat16 or wider, within the bound.
No kernel may reach another device: no remote copies, remote signals or barrier semaphores. Data moves between devices by JAX's collectives and lax.ppermute only.
A program may use at most 128 MiB of HBM per device.

```python
import math
import jax
import jax.numpy as jnp
from jax import lax

FF = 28672
DW = 4096
BLOCK = 1024
NRB = 4
NCB = 28
NBLK = 112
PIECE = 16
KP = 8
SLOTS = 6
OWNED = 192
N_FSDP = 32
N_GROUP = 8


def draw_owner_table(key, part):
    key = jax.random.fold_in(key, 11)
    key_owner, key_rows, key_order, key_shift = jax.random.split(key, 4)
    share_cap = (NCB + N_FSDP - 2) // (N_FSDP - 1)
    owners = jax.random.permutation(key_owner, N_FSDP).astype(jnp.int32)
    row_rank = jax.random.permutation(key_rows, NRB)
    extra_count = jnp.where(row_rank < NRB // 2, 2 * share_cap, share_cap).astype(jnp.int32)
    scores = jax.random.randint(key_order, (NRB, NCB), 0, 1 << 20) * NCB + jnp.arange(NCB, dtype=jnp.int32)[None, :]
    position = jnp.argsort(jnp.argsort(scores, axis=1, stable=True), axis=1, stable=True).astype(jnp.int32)
    shift_rows = jax.random.randint(key_shift, (NRB, 1), 0, N_FSDP - 1)
    other_owner = 1 + (position - extra_count[:, None] + shift_rows) % (N_FSDP - 1)
    chosen = jnp.where(position < extra_count[:, None], 0, other_owner)
    return owners[chosen].reshape(NBLK).astype(jnp.int32)


def draw_momentum(key, part):
    key = jax.random.fold_in(key, 23)
    key_base, key_rows, key_cols = jax.random.split(key, 3)
    rising = jnp.exp(math.log(3.0) * (jnp.arange(DW, dtype=jnp.float32) / DW - 0.5))
    row_scale = jnp.exp(jax.random.uniform(key_rows, (DW, 1), minval=math.log(0.3), maxval=math.log(3.0))) * rising[:, None]
    col_scale = jnp.exp(jax.random.uniform(key_cols, (1, FF), minval=math.log(0.3), maxval=math.log(3.0)))
    base = jax.random.normal(key_base, (DW, FF))
    return (base * row_scale * col_scale).astype(jnp.float32)


def draw_left_root(key, part):
    key = jax.random.fold_in(key, 37)
    key_diag, key_noise = jax.random.split(key)
    diagonal = jnp.exp(jax.random.uniform(key_diag, (OWNED, BLOCK, 1), minval=math.log(0.3), maxval=math.log(3.0)))
    noise = jax.random.normal(key_noise, (OWNED, BLOCK, BLOCK))
    identity = (jnp.arange(BLOCK)[:, None] == jnp.arange(BLOCK)[None, :]).astype(jnp.float32)
    matrix = identity[None, :, :] * diagonal + noise * (0.8 / math.sqrt(BLOCK))
    return matrix.reshape(OWNED, KP, N_GROUP, PIECE, BLOCK).astype(jnp.bfloat16)


def draw_right_root(key, part):
    key = jax.random.fold_in(key, 41)
    key_diag, key_noise = jax.random.split(key)
    diagonal = jnp.exp(jax.random.uniform(key_diag, (OWNED, 1, BLOCK), minval=math.log(0.3), maxval=math.log(3.0)))
    noise = jax.random.normal(key_noise, (OWNED, BLOCK, BLOCK))
    identity = (jnp.arange(BLOCK)[:, None] == jnp.arange(BLOCK)[None, :]).astype(jnp.float32)
    matrix = identity[None, :, :] * diagonal + noise * (0.8 / math.sqrt(BLOCK))
    return matrix.reshape(OWNED, KP, N_GROUP, PIECE, BLOCK).astype(jnp.bfloat16)


def block_levels(rng, dims, pieces, least, high):
    level, own = 1.0, jax.random.fold_in(rng, 6)
    for axis_at, shards_of in pieces:
        draws = jnp.exp(jax.random.uniform(jax.random.fold_in(own, axis_at), (shards_of,), jnp.float32, least / len(pieces), high / len(pieces)))
        level = level * jnp.repeat(draws, dims[axis_at] // shards_of).reshape([-1 if axis == axis_at else 1 for axis in range(len(dims))])
    return level


def normal_values(key, extent, spread, most, cuts=(), held_as=jnp.bfloat16):
    array = jax.random.normal(key, extent, jnp.float32) * spread
    if len(cuts) > 0:
        array = block_levels(key, extent, cuts, -0.22, 0.18) * array
    return jnp.clip(array, min=-most, max=most).astype(held_as)


def setup_inputs(seed: int = 0) -> dict:
    key_of = jax.random.split(jax.random.key(seed), 7)
    return {
        "grad": normal_values(key_of[0], (DW, FF), 1.0, 6.0, ((0, 256),)),
        "momentum": draw_momentum(jax.random.fold_in(key_of[6], 71), 0),
        "second": jnp.clip(jnp.exp(math.log(5.0) - 3.218876 * jax.random.uniform(key_of[2], (DW, FF), jnp.float32) ** block_levels(key_of[2], (DW, FF), ((0, 256),), -0.2, 0.2)), 0.2, 5.0),
        "left_root": draw_left_root(jax.random.fold_in(key_of[6], 71), 0),
        "right_root": draw_right_root(jax.random.fold_in(key_of[6], 71), 0),
        "owner_table": draw_owner_table(jax.random.fold_in(key_of[6], 71), 0),
    }


def grouped_product(rows_left, rows_right):
    left_parts = rows_left.astype(jnp.float32).reshape(KP, N_GROUP, PIECE, BLOCK)
    right_parts = rows_right.astype(jnp.float32).reshape(KP, N_GROUP, PIECE, BLOCK)
    partial_value = jnp.einsum('kgpi,kgpj->gij', left_parts, right_parts)
    rounded = lax.optimization_barrier(partial_value.astype(jnp.bfloat16))
    return lax.optimization_barrier(jnp.sum(rounded.astype(jnp.float32), axis=0))

def reference(grad, momentum, second, left_root, right_root, owner_table):
    grad_wide = grad.astype(jnp.float32)
    new_momentum = 0.9 * momentum + 0.1 * grad_wide
    new_second = 0.95 * second + 0.05 * grad_wide * grad_wide
    adam_dir = new_momentum / (jnp.sqrt(new_second) + 1e-08)
    adam_sq = lax.optimization_barrier(jnp.sum(jnp.square(adam_dir).reshape(NRB, BLOCK, NCB, BLOCK), axis=(1, 3))).reshape(NBLK)
    sent_rows = new_momentum.astype(jnp.bfloat16)
    blocks = sent_rows.reshape(NRB, BLOCK, NCB, BLOCK).transpose(0, 2, 1, 3).reshape(NBLK, BLOCK, BLOCK)
    numbers = jnp.arange(NBLK, dtype=jnp.int32)
    earlier = (numbers[None, :] < numbers[:, None]) & (owner_table[None, :] == owner_table[:, None])
    slot_of = lax.optimization_barrier(jnp.sum(earlier.astype(jnp.int32), axis=1)).astype(jnp.int32)
    factor_index = (owner_table * SLOTS + slot_of).astype(jnp.int32)
    left_all = left_root.reshape(OWNED, BLOCK, BLOCK)
    right_all = right_root.reshape(OWNED, BLOCK, BLOCK)

    def precondition(slot_item):
        moment_block, factor_pick, adam_total = slot_item
        left_one = lax.dynamic_index_in_dim(left_all, factor_pick, 0, keepdims=False)
        right_one = lax.dynamic_index_in_dim(right_all, factor_pick, 0, keepdims=False)
        crossed = grouped_product(moment_block, left_one).astype(jnp.bfloat16)
        shaped = grouped_product(crossed, right_one)
        shampoo_sq = jnp.sum(shaped * shaped)
        graft_ratio = jnp.sqrt(adam_total / (shampoo_sq + 1e-06))
        return (graft_ratio * shaped).astype(jnp.bfloat16)
    updates = lax.map(precondition, (blocks, factor_index, adam_sq))
    update = updates.reshape(NRB, NCB, BLOCK, BLOCK).transpose(0, 2, 1, 3).reshape(DW, FF)
    return (update, new_momentum, new_second)
```

```python
import jax
import jax.numpy as jnp
from jax import lax
from jax.experimental import pallas as pl
from jax.experimental.pallas import tpu as pltpu
from jax.sharding import PartitionSpec as P

NRB = 4
NCB = 28
NBLK = NRB * NCB
KP = 8
SLOTS = 6
N_FSDP = 32
N_GROUP = 8
PIECE = 16
BLOCK = 1024
ROWS = KP * PIECE
TAIL = 128
WIDE = 2 * BLOCK + TAIL
CPS = 4
SLOT_HOME = (0, 2, 4, 6, 1, 5)
MOVES = ((0, 0), (0, 1), (1, 0), (1, 1), (3, 0), (3, 1), (2, 0), (2, 1))
BF16 = jnp.bfloat16
F32 = jnp.float32


def to_device(g, move):
    dy, flip = move
    return ((g // 2 + dy) % 4) * 2 + ((g % 2 + flip) % 2)


def from_device(g, move):
    dy, flip = move
    return ((g // 2 + 4 - dy) % 4) * 2 + ((g % 2 + flip) % 2)


def has_slot(g):
    return (g % 2 == 0) | (g % 4 == 1)


def slot_at(g):
    return jnp.where(g % 2 == 0, g // 2, 4 + g // 4)


def pairs_in(move):
    return [(i, to_device(i, move)) for i in range(N_GROUP) if to_device(i, move) in SLOT_HOME]


def pairs_out(move):
    return [(i, to_device(i, move)) for i in range(N_GROUP) if i in SLOT_HOME]


def split3(total):
    first = total.astype(BF16).astype(F32)
    rest = total - first
    second = rest.astype(BF16).astype(F32)
    return first, second, rest - second


def adam_kernel(table, grad, momentum, second, new_momentum, new_second, packed, count):
    step = pl.program_id(0)
    row_block = lax.axis_index("fsdp") // KP

    @pl.when(step == 0)
    def _():
        packed[...] = jnp.zeros_like(packed)

        def clear(i, c):
            count[i] = 0
            return c

        lax.fori_loop(0, N_FSDP, clear, 0)

    rows = lax.broadcasted_iota(jnp.int32, (PIECE, TAIL), 0)
    for j in range(CPS):
        lanes = pl.ds(j * BLOCK, BLOCK)
        wide = grad[:, lanes].astype(F32)
        moment = 0.9 * momentum[:, lanes] + 0.1 * wide
        square = 0.95 * second[:, lanes] + 0.05 * wide * wide
        new_momentum[:, lanes] = moment
        new_second[:, lanes] = square
        direction = moment / (jnp.sqrt(square) + 1e-08)
        total = jnp.sum(jnp.sum(direction * direction, axis=0, keepdims=True), axis=1, keepdims=True)
        owner = table[row_block * NCB + step * CPS + j]
        place = count[owner]
        count[owner] = place + 1
        packed[owner, :, pl.ds(pl.multiple_of(place * BLOCK, BLOCK), BLOCK)] = moment.astype(BF16)
        first, middle, last = split3(jnp.broadcast_to(total, (PIECE, TAIL)))
        at = rows - place * 8
        tile = jnp.where(at == 0, first, jnp.where(at == 1, middle, jnp.where(at == 2, last, 0.0)))
        tail = packed[owner, :, 2 * BLOCK :].astype(F32)
        packed[owner, :, 2 * BLOCK :] = (tail + tile).astype(BF16)


def adam_pack(grad, momentum, second, table):
    width = CPS * BLOCK
    spec = pl.BlockSpec((PIECE, width), lambda i, t: (0, i))
    return pl.pallas_call(
        adam_kernel,
        grid_spec=pltpu.PrefetchScalarGridSpec(
            num_scalar_prefetch=1,
            grid=(NCB // CPS,),
            in_specs=[spec, spec, spec],
            out_specs=[spec, spec, pl.BlockSpec((N_FSDP, PIECE, WIDE), lambda i, t: (0, 0, 0))],
            scratch_shapes=[pltpu.SMEM((N_FSDP,), jnp.int32)],
        ),
        out_shape=[
            jax.ShapeDtypeStruct(momentum.shape, F32),
            jax.ShapeDtypeStruct(second.shape, F32),
            jax.ShapeDtypeStruct((N_FSDP, PIECE, WIDE), BF16),
        ],
        compiler_params=pltpu.CompilerParams(vmem_limit_bytes=32 << 20),
    )(table, grad, momentum, second)


def find_slots(table, me, where):
    for s in range(SLOTS):
        where[2 * s] = 0
        where[2 * s + 1] = 0

    def per_row(rb, slot):
        def per_block(cb, carry):
            slot, place = carry
            hit = table[rb * NCB + cb] == me

            @pl.when(hit)
            def _():
                where[2 * slot] = rb
                where[2 * slot + 1] = place

            add = hit.astype(jnp.int32)
            return slot + add, place + add

        return lax.fori_loop(0, NCB, per_block, (slot, jnp.int32(0)))[0]

    return lax.fori_loop(0, NRB, per_row, jnp.int32(0))


def collect_kernel(table, arrived, *refs):
    outs, where = refs[:8], refs[8]
    group = lax.axis_index("group")
    find_slots(table, lax.axis_index("fsdp"), where)
    rows = lax.broadcasted_iota(jnp.int32, (PIECE, TAIL), 0)
    for move, out in zip(MOVES, outs):
        dest = to_device(group, move)

        @pl.when(has_slot(dest))
        def _():
            slot = slot_at(dest)
            row_block = where[2 * slot]
            place = where[2 * slot + 1]
            lanes = pl.ds(pl.multiple_of(place * BLOCK, BLOCK), BLOCK)
            total = jnp.zeros((PIECE, TAIL), F32)
            for k in range(KP):
                out[k * PIECE : (k + 1) * PIECE, :] = arrived[row_block * KP + k, :, lanes]
                total += arrived[row_block * KP + k, :, 2 * BLOCK :].astype(F32)
            total = jnp.sum(jnp.where(rows // 8 == place, total, 0.0), axis=0, keepdims=True)
            first, middle, last = split3(jnp.broadcast_to(total, (PIECE, TAIL)))
            tile = jnp.where(rows == 0, first, jnp.where(rows == 1, middle, jnp.where(rows == 2, last, 0.0)))
            tile = tile.astype(BF16)
            for part in range(BLOCK // TAIL):
                out[ROWS : ROWS + PIECE, part * TAIL : (part + 1) * TAIL] = tile


def collect(arrived, table):
    return pl.pallas_call(
        collect_kernel,
        in_specs=[pl.BlockSpec(memory_space=pltpu.SMEM), pl.BlockSpec(memory_space=pltpu.VMEM)],
        out_specs=[pl.BlockSpec(memory_space=pltpu.VMEM)] * 8,
        out_shape=[jax.ShapeDtypeStruct((ROWS + PIECE, BLOCK), BF16)] * 8,
        scratch_shapes=[pltpu.SMEM((2 * SLOTS,), jnp.int32)],
        compiler_params=pltpu.CompilerParams(vmem_limit_bytes=32 << 20),
    )(table, arrived)


def factor_kernel(left, right, *refs):
    outs, sem = refs[:7], refs[7]
    group = lax.axis_index("group")
    for go in (True, False):
        for n, move in enumerate(MOVES[1:]):
            dest = to_device(group, move)

            @pl.when(has_slot(dest))
            def _():
                slot = slot_at(dest)
                for m, source in enumerate((left, right)):
                    copy = pltpu.make_async_copy(source.at[slot], outs[n].at[m], sem.at[n, m])
                    if go:
                        copy.start()
                    else:
                        copy.wait()


def factor_rows(left, right):
    return pl.pallas_call(
        factor_kernel,
        in_specs=[pl.BlockSpec(memory_space=pl.ANY)] * 2,
        out_specs=[pl.BlockSpec(memory_space=pltpu.VMEM)] * 7,
        out_shape=[jax.ShapeDtypeStruct((2, KP, PIECE, BLOCK), BF16)] * 7,
        scratch_shapes=[pltpu.SemaphoreType.DMA((7, 2))],
        compiler_params=pltpu.CompilerParams(vmem_limit_bytes=32 << 20),
    )(left, right)


def product_kernel(*refs):
    moments, factors = refs[:8], refs[8:15]
    left, right = refs[15:17]
    outs = refs[17:25]
    left_all, right_all, moment_all, tail_all, crossed, shaped, sem = refs[25:]
    group = lax.axis_index("group")

    @pl.when(has_slot(group))
    def _():
        slot = slot_at(group)
        copies = []
        for n, move in enumerate(MOVES):
            source = from_device(group, move)
            left_rows = left.at[slot] if n == 0 else factors[n - 1].at[0]
            right_rows = right.at[slot] if n == 0 else factors[n - 1].at[1]
            copies.append((
                pltpu.make_async_copy(left_rows, left_all.at[:, source], sem.at[0, n]),
                pltpu.make_async_copy(right_rows, right_all.at[:, source], sem.at[1, n]),
                pltpu.make_async_copy(moments[n].at[:KP], moment_all.at[:, source], sem.at[2, n]),
                pltpu.make_async_copy(moments[n].at[KP, :, :TAIL], tail_all.at[n], sem.at[3, n]),
            ))
        for part in (0, 2, 3, 1):
            for c in copies:
                c[part].start()
        for part in (0, 2, 3):
            for c in copies:
                c[part].wait()
        tail = jnp.zeros((PIECE, TAIL), F32)
        for n in range(8):
            tail += tail_all[n].astype(F32)
        adam_sq = jnp.sum(tail, axis=0, keepdims=True)[:, :1]
        moment = moment_all[...].reshape(BLOCK, BLOCK)
        step = 256
        for part in range(BLOCK // step):
            chunk = left_all[:, :, :, part * step : (part + 1) * step].reshape(BLOCK, step)
            crossed[part * step : (part + 1) * step, :] = lax.dot_general(
                chunk, moment, (((0,), (0,)), ((), ())), preferred_element_type=F32
            ).astype(BF16)
        for c in copies:
            c[1].wait()
        factor = right_all[...].reshape(BLOCK, BLOCK)
        total = jnp.zeros((1, BLOCK), F32)
        for part in range(BLOCK // step):
            value = jnp.dot(
                crossed[part * step : (part + 1) * step, :], factor, preferred_element_type=F32
            )
            shaped[part * step : (part + 1) * step, :] = value
            total += jnp.sum(value * value, axis=0, keepdims=True)
        shampoo_sq = jnp.sum(total, axis=1, keepdims=True)
        ratio = jnp.sqrt(adam_sq / (shampoo_sq + 1e-06))
        for n, move in enumerate(MOVES):
            dest = to_device(group, move)
            for k in range(KP):
                rows = pl.ds(pl.multiple_of(k * ROWS + dest * PIECE, PIECE), PIECE)
                outs[n][k * PIECE : (k + 1) * PIECE, :] = (ratio * shaped[rows, :]).astype(BF16)


def product(moments, factors, left, right):
    whole = pltpu.VMEM((KP, N_GROUP, PIECE, BLOCK), BF16)
    return pl.pallas_call(
        product_kernel,
        in_specs=[pl.BlockSpec(memory_space=pl.ANY)] * 17,
        out_specs=[pl.BlockSpec(memory_space=pltpu.VMEM)] * 8,
        out_shape=[jax.ShapeDtypeStruct((ROWS, BLOCK), BF16)] * 8,
        scratch_shapes=[
            whole,
            whole,
            whole,
            pltpu.VMEM((N_GROUP, PIECE, TAIL), BF16),
            pltpu.VMEM((BLOCK, BLOCK), BF16),
            pltpu.VMEM((BLOCK, BLOCK), F32),
            pltpu.SemaphoreType.DMA((4, 8)),
        ],
        compiler_params=pltpu.CompilerParams(vmem_limit_bytes=48 << 20),
    )(*moments, *factors, left, right)


def return_kernel(table, *refs):
    parts, out, where = refs[:8], refs[8], refs[9]
    group = lax.axis_index("group")
    used = find_slots(table, lax.axis_index("fsdp"), where)
    for move, part in zip(MOVES, parts):
        source = from_device(group, move)
        slot = slot_at(source)

        @pl.when(has_slot(source) & (slot < used))
        def _():
            row_block = where[2 * slot]
            place = where[2 * slot + 1]
            lanes = pl.ds(pl.multiple_of(place * BLOCK, BLOCK), BLOCK)
            for k in range(KP):
                out[row_block * KP + k, :, lanes] = part[k * PIECE : (k + 1) * PIECE, :]


def return_pack(parts, table):
    return pl.pallas_call(
        return_kernel,
        in_specs=[pl.BlockSpec(memory_space=pltpu.SMEM)] + [pl.BlockSpec(memory_space=pltpu.VMEM)] * 8,
        out_specs=pl.BlockSpec(memory_space=pltpu.VMEM),
        out_shape=jax.ShapeDtypeStruct((N_FSDP, PIECE, 2 * BLOCK), BF16),
        scratch_shapes=[pltpu.SMEM((2 * SLOTS,), jnp.int32)],
        compiler_params=pltpu.CompilerParams(vmem_limit_bytes=32 << 20),
    )(table, *parts)


def place_kernel(table, arrived, out, count):
    row_block = lax.axis_index("fsdp") // KP
    for i in range(N_FSDP):
        count[i] = 0
    for cb in range(NCB):
        owner = table[row_block * NCB + cb]
        place = count[owner]
        count[owner] = place + 1
        lanes = pl.ds(pl.multiple_of(place * BLOCK, BLOCK), BLOCK)
        out[:, cb * BLOCK : (cb + 1) * BLOCK] = arrived[owner, :, lanes]


def place_rows(arrived, table):
    return pl.pallas_call(
        place_kernel,
        in_specs=[pl.BlockSpec(memory_space=pltpu.SMEM), pl.BlockSpec(memory_space=pltpu.VMEM)],
        out_specs=pl.BlockSpec(memory_space=pltpu.VMEM),
        out_shape=jax.ShapeDtypeStruct((PIECE, NCB * BLOCK), BF16),
        scratch_shapes=[pltpu.SMEM((N_FSDP,), jnp.int32)],
        compiler_params=pltpu.CompilerParams(vmem_limit_bytes=32 << 20),
    )(table, arrived)


def body(grad, momentum, second, left_root, right_root, owner_table):
    left = left_root.reshape(SLOTS, KP, PIECE, BLOCK)
    right = right_root.reshape(SLOTS, KP, PIECE, BLOCK)
    new_momentum, new_second, packed = adam_pack(grad, momentum, second, owner_table)
    factors = [
        lax.ppermute(rows, "group", pairs_in(move))
        for rows, move in zip(factor_rows(left, right), MOVES[1:])
    ]
    arrived = lax.all_to_all(packed, "fsdp", split_axis=0, concat_axis=0, tiled=True)
    sent = collect(arrived, owner_table)
    moments = [sent[0]] + [
        lax.ppermute(rows, "group", pairs_in(move)) for rows, move in zip(sent[1:], MOVES[1:])
    ]
    moments = [rows.reshape(KP + 1, PIECE, BLOCK) for rows in moments]
    shaped = product(moments, factors, left, right)
    parts = [shaped[0]] + [
        lax.ppermute(rows, "group", pairs_out(move)) for rows, move in zip(shaped[1:], MOVES[1:])
    ]
    returning = return_pack(parts, owner_table)
    arriving = lax.all_to_all(returning, "fsdp", split_axis=0, concat_axis=0, tiled=True)
    return place_rows(arriving, owner_table), new_momentum, new_second


def solution(mesh):
    rows = P(("fsdp", "group"), None)
    factors = P("fsdp", None, "group", None, None)
    return jax.shard_map(
        body,
        mesh=mesh,
        in_specs=(rows, rows, rows, factors, factors, P()),
        out_specs=(rows, rows, rows),
        check_vma=False,
    )
```

```python
import jax
import jax.numpy as jnp
from jax import lax
from jax.experimental import pallas as pl
from jax.experimental.pallas import tpu as pltpu
from jax.sharding import PartitionSpec as P

NRB = 4
NCB = 28
NBLK = NRB * NCB
KP = 8
SLOTS = 6
N_FSDP = 32
N_GROUP = 8
PIECE = 16
BLOCK = 1024
ROWS = KP * PIECE
TAIL = 128
CPS = 7
EARLY = 3
HELD = 7
SLOT_HOME = (0, 2, 4, 6, 1, 5)
MOVES = ((0, 0), (2, 0), (1, 0), (3, 0), (2, 1), (1, 1), (3, 1), (0, 1))
BF16 = jnp.bfloat16
F32 = jnp.float32


def to_device(g, move):
    dy, flip = move
    return ((g // 2 + dy) % 4) * 2 + ((g % 2 + flip) % 2)


def from_device(g, move):
    dy, flip = move
    return ((g // 2 + 4 - dy) % 4) * 2 + ((g % 2 + flip) % 2)


def has_slot(g):
    return (g % 2 == 0) | (g % 4 == 1)


def slot_at(g):
    return jnp.where(g % 2 == 0, g // 2, 4 + g // 4)


def pairs_in(move):
    return [(i, to_device(i, move)) for i in range(N_GROUP) if to_device(i, move) in SLOT_HOME]


def pairs_out(move):
    return [(i, to_device(i, move)) for i in range(N_GROUP) if i in SLOT_HOME]


def factor_copies(moves, left, right, outs, sem, go):
    group = lax.axis_index("group")
    for n, move in enumerate(moves):
        dest = to_device(group, move)

        @pl.when(has_slot(dest))
        def _():
            slot = slot_at(dest)
            for m, source in enumerate((left, right)):
                copy = pltpu.make_async_copy(source.at[slot], outs[n].at[m], sem.at[n, m])
                if go:
                    copy.start()
                else:
                    copy.wait()


def pack_kernel(table, grad, momentum, left, right, packed, *refs):
    rows, count, sem = refs[:EARLY], refs[EARLY], refs[EARLY + 1]
    moves = MOVES[1 : EARLY + 1]
    step = pl.program_id(0)
    row_block = lax.axis_index("fsdp") // KP

    @pl.when(step == 0)
    def _():
        factor_copies(moves, left, right, rows, sem, True)
        for i in range(N_FSDP):
            count[i] = 0

    @pl.when(step == pl.num_programs(0) - 1)
    def _():
        factor_copies(moves, left, right, rows, sem, False)

    for j in range(CPS):
        lanes = pl.ds(j * BLOCK, BLOCK)
        moment = 0.9 * momentum[:, lanes] + 0.1 * grad[:, lanes].astype(F32)
        owner = table[row_block * NCB + step * CPS + j]
        place = count[owner]
        count[owner] = place + 1
        packed[owner, :, pl.ds(pl.multiple_of(place * BLOCK, BLOCK), BLOCK)] = moment.astype(BF16)


def pack_rows(grad, momentum, left, right, table):
    spec = pl.BlockSpec((PIECE, CPS * BLOCK), lambda i, t: (0, i))
    anywhere = pl.BlockSpec(memory_space=pl.ANY)
    rows = (2, KP, PIECE, BLOCK)
    outs = pl.pallas_call(
        pack_kernel,
        grid_spec=pltpu.PrefetchScalarGridSpec(
            num_scalar_prefetch=1,
            grid=(NCB // CPS,),
            in_specs=[spec, spec, anywhere, anywhere],
            out_specs=[pl.BlockSpec((N_FSDP, PIECE, 2 * BLOCK), lambda i, t: (0, 0, 0))]
            + [pl.BlockSpec(rows, lambda i, t: (0, 0, 0, 0))] * EARLY,
            scratch_shapes=[pltpu.SMEM((N_FSDP,), jnp.int32), pltpu.SemaphoreType.DMA((EARLY, 2))],
        ),
        out_shape=[jax.ShapeDtypeStruct((N_FSDP, PIECE, 2 * BLOCK), BF16)]
        + [jax.ShapeDtypeStruct(rows, BF16)] * EARLY,
        compiler_params=pltpu.CompilerParams(vmem_limit_bytes=60 << 20),
    )(table, grad, momentum, left, right)
    return outs[0], outs[1:]


def state_kernel(grad, momentum, second, new_momentum, new_second, sums):
    step = pl.program_id(0)

    @pl.when(step == 0)
    def _():
        sums[...] = jnp.zeros_like(sums)

    lane = lax.broadcasted_iota(jnp.int32, sums.shape, 1)
    for j in range(CPS):
        lanes = pl.ds(j * BLOCK, BLOCK)
        wide = grad[:, lanes].astype(F32)
        moment = 0.9 * momentum[:, lanes] + 0.1 * wide
        square = 0.95 * second[:, lanes] + 0.05 * wide * wide
        new_momentum[:, lanes] = moment
        new_second[:, lanes] = square
        direction = moment / (jnp.sqrt(square) + 1e-08)
        total = jnp.sum(jnp.sum(direction * direction, axis=0, keepdims=True), axis=1, keepdims=True)
        sums[...] += jnp.where(lane == step * CPS + j, total, 0.0)


def update_states(grad, momentum, second):
    spec = pl.BlockSpec((PIECE, CPS * BLOCK), lambda i: (0, i))
    return pl.pallas_call(
        state_kernel,
        grid=(NCB // CPS,),
        in_specs=[spec, spec, spec],
        out_specs=[spec, spec, pl.BlockSpec((8, TAIL), lambda i: (0, 0))],
        out_shape=[
            jax.ShapeDtypeStruct(momentum.shape, F32),
            jax.ShapeDtypeStruct(second.shape, F32),
            jax.ShapeDtypeStruct((8, TAIL), F32),
        ],
        compiler_params=pltpu.CompilerParams(vmem_limit_bytes=60 << 20),
    )(grad, momentum, second)


def find_slots(table, me, where):
    for s in range(SLOTS):
        where[2 * s] = 0
        where[2 * s + 1] = 0

    def per_row(rb, slot):
        def per_block(cb, carry):
            slot, place = carry
            hit = table[rb * NCB + cb] == me

            @pl.when(hit)
            def _():
                where[2 * slot] = rb
                where[2 * slot + 1] = place

            add = hit.astype(jnp.int32)
            return slot + add, place + add

        return lax.fori_loop(0, NCB, per_block, (slot, jnp.int32(0)))[0]

    where[2 * SLOTS] = lax.fori_loop(0, NRB, per_row, jnp.int32(0))


def collect_kernel(where, arrived, *outs):
    group = lax.axis_index("group")
    for move, out in zip(MOVES, outs):
        dest = to_device(group, move)

        @pl.when(has_slot(dest))
        def _():
            slot = slot_at(dest)
            row_block = where[2 * slot]
            place = where[2 * slot + 1]
            lanes = pl.ds(pl.multiple_of(place * BLOCK, BLOCK), BLOCK)
            for k in range(KP):
                out[k] = arrived[row_block * KP + k, :, lanes]


def collect(arrived, where):
    return pl.pallas_call(
        collect_kernel,
        in_specs=[pl.BlockSpec(memory_space=pltpu.SMEM), pl.BlockSpec(memory_space=pltpu.VMEM)],
        out_specs=[pl.BlockSpec(memory_space=pltpu.VMEM)] * 8,
        out_shape=[jax.ShapeDtypeStruct((KP, PIECE, BLOCK), BF16)] * 8,
        compiler_params=pltpu.CompilerParams(vmem_limit_bytes=32 << 20),
    )(where, arrived)


def factor_kernel(table, left, right, *refs):
    outs, where, sem = refs[: 7 - EARLY], refs[7 - EARLY], refs[8 - EARLY]
    moves = MOVES[EARLY + 1 :]
    factor_copies(moves, left, right, outs, sem, True)
    find_slots(table, lax.axis_index("fsdp"), where)
    factor_copies(moves, left, right, outs, sem, False)


def factor_rows(left, right, table):
    late = 7 - EARLY
    outs = pl.pallas_call(
        factor_kernel,
        in_specs=[pl.BlockSpec(memory_space=pltpu.SMEM)] + [pl.BlockSpec(memory_space=pl.ANY)] * 2,
        out_specs=[pl.BlockSpec(memory_space=pltpu.VMEM)] * late + [pl.BlockSpec(memory_space=pltpu.SMEM)],
        out_shape=[jax.ShapeDtypeStruct((2, KP, PIECE, BLOCK), BF16)] * late
        + [jax.ShapeDtypeStruct((2 * SLOTS + 1,), jnp.int32)],
        scratch_shapes=[pltpu.SemaphoreType.DMA((late, 2))],
        compiler_params=pltpu.CompilerParams(vmem_limit_bytes=60 << 20),
    )(table, left, right)
    return outs[:late], outs[late]


def product_kernel(*refs):
    moments, factors = refs[:8], refs[8:15]
    left, right = refs[15:17]
    outs = refs[17:25]
    left_all, right_all, moment_all, crossed, shaped, sem = refs[25:]
    group = lax.axis_index("group")

    @pl.when(has_slot(group))
    def _():
        slot = slot_at(group)
        copies = []
        for n, move in enumerate(MOVES):
            source = from_device(group, move)
            left_rows = left.at[slot] if n == 0 else factors[n - 1].at[0]
            right_rows = right.at[slot] if n == 0 else factors[n - 1].at[1]
            copies.append((
                pltpu.make_async_copy(left_rows, left_all.at[:, source], sem.at[0, n]),
                pltpu.make_async_copy(right_rows, right_all.at[:, source], sem.at[1, n]),
                pltpu.make_async_copy(moments[n], moment_all.at[:, source], sem.at[2, n]),
            ))
        for part in (0, 2, 1):
            for c in copies:
                c[part].start()
        for part in (0, 2):
            for c in copies:
                c[part].wait()
        moment = moment_all[...].reshape(BLOCK, BLOCK)
        step = 256
        for part in range(BLOCK // step):
            chunk = left_all[:, :, :, part * step : (part + 1) * step].reshape(BLOCK, step)
            crossed[part * step : (part + 1) * step, :] = lax.dot_general(
                chunk, moment, (((0,), (0,)), ((), ())), preferred_element_type=F32
            ).astype(BF16)
        for c in copies:
            c[1].wait()
        factor = right_all[...].reshape(BLOCK, BLOCK)
        total = jnp.zeros((1, BLOCK), F32)
        for part in range(BLOCK // step):
            value = jnp.dot(
                crossed[part * step : (part + 1) * step, :], factor, preferred_element_type=F32
            )
            shaped[part * step : (part + 1) * step, :] = value
            total += jnp.sum(value * value, axis=0, keepdims=True)
        shampoo_sq = jnp.sum(total, axis=1, keepdims=True)
        scale = 1.0 / jnp.sqrt(shampoo_sq + 1e-06)
        for n, move in enumerate(MOVES):
            dest = to_device(group, move)
            for k in range(KP):
                rows = pl.ds(pl.multiple_of(k * ROWS + dest * PIECE, PIECE), PIECE)
                outs[n][k] = (scale * shaped[rows, :]).astype(BF16)


def product(moments, factors, left, right):
    whole = pltpu.VMEM((KP, N_GROUP, PIECE, BLOCK), BF16)
    return pl.pallas_call(
        product_kernel,
        in_specs=[pl.BlockSpec(memory_space=pl.ANY)] * 17,
        out_specs=[pl.BlockSpec(memory_space=pltpu.VMEM)] * 8,
        out_shape=[jax.ShapeDtypeStruct((KP, PIECE, BLOCK), BF16)] * 8,
        scratch_shapes=[
            whole,
            whole,
            whole,
            pltpu.VMEM((BLOCK, BLOCK), BF16),
            pltpu.VMEM((BLOCK, BLOCK), F32),
            pltpu.SemaphoreType.DMA((3, 8)),
        ],
        compiler_params=pltpu.CompilerParams(vmem_limit_bytes=48 << 20),
    )(*moments, *factors, left, right)


def return_kernel(where, *refs):
    parts, out = refs[:8], refs[8]
    group = lax.axis_index("group")
    used = where[2 * SLOTS]
    for move, part in zip(MOVES, parts):
        source = from_device(group, move)
        slot = slot_at(source)

        @pl.when(has_slot(source) & (slot < used))
        def _():
            row_block = where[2 * slot]
            place = where[2 * slot + 1]
            lanes = pl.ds(pl.multiple_of(place * BLOCK, BLOCK), BLOCK)
            for k in range(KP):
                out[row_block * KP + k, :, lanes] = part[k]


def return_pack(parts, where):
    return pl.pallas_call(
        return_kernel,
        in_specs=[pl.BlockSpec(memory_space=pltpu.SMEM)] + [pl.BlockSpec(memory_space=pltpu.VMEM)] * 8,
        out_specs=pl.BlockSpec(memory_space=pltpu.VMEM),
        out_shape=jax.ShapeDtypeStruct((N_FSDP, PIECE, 2 * BLOCK), BF16),
        compiler_params=pltpu.CompilerParams(vmem_limit_bytes=32 << 20),
    )(where, *parts)


def place_kernel(table, sums, arrived, out, count):
    row_block = lax.axis_index("fsdp") // KP
    for i in range(N_FSDP):
        count[i] = 0
    root = jnp.sqrt(sums[...])
    for cb in range(NCB):
        owner = table[row_block * NCB + cb]
        place = count[owner]
        count[owner] = place + 1
        lanes = pl.ds(pl.multiple_of(place * BLOCK, BLOCK), BLOCK)
        rows = arrived[owner, :, lanes].astype(F32)
        out[:, cb * BLOCK : (cb + 1) * BLOCK] = (root[:1, cb : cb + 1] * rows).astype(BF16)


def place_rows(arrived, sums, table):
    return pl.pallas_call(
        place_kernel,
        in_specs=[pl.BlockSpec(memory_space=pltpu.SMEM)] + [pl.BlockSpec(memory_space=pltpu.VMEM)] * 2,
        out_specs=pl.BlockSpec(memory_space=pltpu.VMEM),
        out_shape=jax.ShapeDtypeStruct((PIECE, NCB * BLOCK), BF16),
        scratch_shapes=[pltpu.SMEM((N_FSDP,), jnp.int32)],
        compiler_params=pltpu.CompilerParams(vmem_limit_bytes=32 << 20),
    )(table, sums, arrived)


def move_in(rows, move):
    return lax.ppermute(rows, "group", pairs_in(move))


def move_out(rows, move):
    return lax.ppermute(rows, "group", pairs_out(move))


def add_from(sums, axis, bit):
    return sums + lax.ppermute(sums, axis, [(i, i ^ bit) for i in range(lax.axis_size(axis))])


def body(grad, momentum, second, left_root, right_root, owner_table):
    tie = lax.optimization_barrier
    left = left_root.reshape(SLOTS, KP, PIECE, BLOCK)
    right = right_root.reshape(SLOTS, KP, PIECE, BLOCK)
    packed, early = pack_rows(grad, momentum, left, right, owner_table)
    second, left, packed = tie((second, left, packed))
    arrived = lax.all_to_all(packed, "fsdp", split_axis=0, concat_axis=0, tiled=True)
    late, where = factor_rows(left, right, owner_table)
    factors = [move_in(r, m) for r, m in zip(list(early) + list(late), MOVES[1:])]
    new_momentum, new_second, sums = update_states(grad, momentum, second)
    arrived, waited, sums = tie((arrived, factors[:HELD], sums))
    factors = list(waited) + factors[HELD:]
    sent = collect(arrived, where)
    moments = [sent[0]] + [move_in(r, m) for r, m in zip(sent[1:], MOVES[1:])]
    moments, sums = tie((moments, add_from(sums, "fsdp", 1)))
    shaped = product(moments, factors, left, right)
    sums = add_from(sums, "fsdp", 2)
    parts = [shaped[0]] + [move_out(r, m) for r, m in zip(shaped[1:], MOVES[1:])]
    parts[1], sums = tie((parts[1], sums))
    sums = add_from(sums, "fsdp", 4)
    returning = return_pack(parts, where)
    returning, sums = tie((returning, sums))
    arriving = lax.all_to_all(returning, "fsdp", split_axis=0, concat_axis=0, tiled=True)
    for bit in (1, 2, 4):
        sums = add_from(sums, "group", bit)
    return place_rows(arriving, sums, owner_table), new_momentum, new_second


def solution(mesh):
    rows = P(("fsdp", "group"), None)
    factors = P("fsdp", None, "group", None, None)
    return jax.shard_map(
        body,
        mesh=mesh,
        in_specs=(rows, rows, rows, factors, factors, P()),
        out_specs=(rows, rows, rows),
        check_vma=False,
    )
```

```python
import jax
import jax.numpy as jnp
from jax import lax
from jax.experimental import pallas as pl
from jax.experimental.pallas import tpu as pltpu
from jax.sharding import PartitionSpec as P

NRB = 4
NCB = 28
NBLK = NRB * NCB
KP = 8
SLOTS = 6
N_FSDP = 32
N_GROUP = 8
PIECE = 16
BLOCK = 1024
ROWS = KP * PIECE
TAIL = 128
CPS = 7
PACKED = 7
EARLY = 6
HELD = 7
SLOT_HOME = (0, 2, 4, 6, 1, 5)
MOVES = ((0, 0), (2, 0), (1, 0), (3, 0), (2, 1), (1, 1), (3, 1), (0, 1))
BF16 = jnp.bfloat16
F32 = jnp.float32


def to_device(g, move):
    dy, flip = move
    return ((g // 2 + dy) % 4) * 2 + ((g % 2 + flip) % 2)


def from_device(g, move):
    dy, flip = move
    return ((g // 2 + 4 - dy) % 4) * 2 + ((g % 2 + flip) % 2)


def has_slot(g):
    return (g % 2 == 0) | (g % 4 == 1)


def slot_at(g):
    return jnp.where(g % 2 == 0, g // 2, 4 + g // 4)


def pairs_in(move):
    return [(i, to_device(i, move)) for i in range(N_GROUP) if to_device(i, move) in SLOT_HOME]


def pairs_out(move):
    return [(i, to_device(i, move)) for i in range(N_GROUP) if i in SLOT_HOME]


def factor_copies(moves, left, right, outs, sem, go):
    group = lax.axis_index("group")
    for n, move in enumerate(moves):
        dest = to_device(group, move)

        @pl.when(has_slot(dest))
        def _():
            slot = slot_at(dest)
            for m, source in enumerate((left, right)):
                copy = pltpu.make_async_copy(source.at[slot], outs[n].at[m], sem.at[n, m])
                if go:
                    copy.start()
                else:
                    copy.wait()


def pack_kernel(table, grad, momentum, left, right, packed, *refs):
    rows, count, sem = refs[:EARLY], refs[EARLY], refs[EARLY + 1]
    moves = MOVES[1 : EARLY + 1]
    step = pl.program_id(0)
    row_block = lax.axis_index("fsdp") // KP

    @pl.when(step == 0)
    def _():
        factor_copies(moves, left, right, rows, sem, True)
        for i in range(N_FSDP):
            count[i] = 0

    @pl.when(step == pl.num_programs(0) - 1)
    def _():
        factor_copies(moves, left, right, rows, sem, False)

    for j in range(PACKED):
        lanes = pl.ds(j * BLOCK, BLOCK)
        moment = 0.9 * momentum[:, lanes] + 0.1 * grad[:, lanes].astype(F32)
        owner = table[row_block * NCB + step * PACKED + j]
        place = count[owner]
        count[owner] = place + 1
        packed[owner, :, pl.ds(pl.multiple_of(place * BLOCK, BLOCK), BLOCK)] = moment.astype(BF16)


def pack_rows(grad, momentum, left, right, table):
    spec = pl.BlockSpec((PIECE, PACKED * BLOCK), lambda i, t: (0, i))
    anywhere = pl.BlockSpec(memory_space=pl.ANY)
    rows = (2, KP, PIECE, BLOCK)
    outs = pl.pallas_call(
        pack_kernel,
        grid_spec=pltpu.PrefetchScalarGridSpec(
            num_scalar_prefetch=1,
            grid=(NCB // PACKED,),
            in_specs=[spec, spec, anywhere, anywhere],
            out_specs=[pl.BlockSpec((N_FSDP, PIECE, 2 * BLOCK), lambda i, t: (0, 0, 0))]
            + [pl.BlockSpec(rows, lambda i, t: (0, 0, 0, 0))] * EARLY,
            scratch_shapes=[pltpu.SMEM((N_FSDP,), jnp.int32), pltpu.SemaphoreType.DMA((EARLY, 2))],
        ),
        out_shape=[jax.ShapeDtypeStruct((N_FSDP, PIECE, 2 * BLOCK), BF16)]
        + [jax.ShapeDtypeStruct(rows, BF16)] * EARLY,
        compiler_params=pltpu.CompilerParams(vmem_limit_bytes=60 << 20),
    )(table, grad, momentum, left, right)
    return outs[0], outs[1:]


def state_kernel(grad, momentum, second, new_momentum, new_second, sums):
    step = pl.program_id(0)

    @pl.when(step == 0)
    def _():
        sums[...] = jnp.zeros_like(sums)

    lane = lax.broadcasted_iota(jnp.int32, sums.shape, 1)
    for j in range(CPS):
        lanes = pl.ds(j * BLOCK, BLOCK)
        wide = grad[:, lanes].astype(F32)
        moment = 0.9 * momentum[:, lanes] + 0.1 * wide
        square = 0.95 * second[:, lanes] + 0.05 * wide * wide
        new_momentum[:, lanes] = moment
        new_second[:, lanes] = square
        direction = moment / (jnp.sqrt(square) + 1e-08)
        total = jnp.sum(jnp.sum(direction * direction, axis=0, keepdims=True), axis=1, keepdims=True)
        sums[...] += jnp.where(lane == step * CPS + j, total, 0.0)


def update_states(grad, momentum, second):
    spec = pl.BlockSpec((PIECE, CPS * BLOCK), lambda i: (0, i))
    return pl.pallas_call(
        state_kernel,
        grid=(NCB // CPS,),
        in_specs=[spec, spec, spec],
        out_specs=[spec, spec, pl.BlockSpec((8, TAIL), lambda i: (0, 0))],
        out_shape=[
            jax.ShapeDtypeStruct(momentum.shape, F32),
            jax.ShapeDtypeStruct(second.shape, F32),
            jax.ShapeDtypeStruct((8, TAIL), F32),
        ],
        compiler_params=pltpu.CompilerParams(vmem_limit_bytes=60 << 20),
    )(grad, momentum, second)


def find_slots(table, me, where):
    for s in range(SLOTS):
        where[2 * s] = 0
        where[2 * s + 1] = 0

    def per_row(rb, slot):
        def per_block(cb, carry):
            slot, place = carry
            hit = table[rb * NCB + cb] == me

            @pl.when(hit)
            def _():
                where[2 * slot] = rb
                where[2 * slot + 1] = place

            add = hit.astype(jnp.int32)
            return slot + add, place + add

        return lax.fori_loop(0, NCB, per_block, (slot, jnp.int32(0)))[0]

    where[2 * SLOTS] = lax.fori_loop(0, NRB, per_row, jnp.int32(0))


def collect_kernel(where, arrived, *outs):
    group = lax.axis_index("group")
    for move, out in zip(MOVES, outs):
        dest = to_device(group, move)

        @pl.when(has_slot(dest))
        def _():
            slot = slot_at(dest)
            row_block = where[2 * slot]
            place = where[2 * slot + 1]
            lanes = pl.ds(pl.multiple_of(place * BLOCK, BLOCK), BLOCK)
            for k in range(KP):
                out[k] = arrived[row_block * KP + k, :, lanes]


def collect(arrived, where):
    return pl.pallas_call(
        collect_kernel,
        in_specs=[pl.BlockSpec(memory_space=pltpu.SMEM), pl.BlockSpec(memory_space=pltpu.VMEM)],
        out_specs=[pl.BlockSpec(memory_space=pltpu.VMEM)] * 8,
        out_shape=[jax.ShapeDtypeStruct((KP, PIECE, BLOCK), BF16)] * 8,
        compiler_params=pltpu.CompilerParams(vmem_limit_bytes=32 << 20),
    )(where, arrived)


def factor_kernel(table, left, right, *refs):
    outs, where, sem = refs[: 7 - EARLY], refs[7 - EARLY], refs[8 - EARLY]
    moves = MOVES[EARLY + 1 :]
    factor_copies(moves, left, right, outs, sem, True)
    find_slots(table, lax.axis_index("fsdp"), where)
    factor_copies(moves, left, right, outs, sem, False)


def factor_rows(left, right, table):
    late = 7 - EARLY
    outs = pl.pallas_call(
        factor_kernel,
        in_specs=[pl.BlockSpec(memory_space=pltpu.SMEM)] + [pl.BlockSpec(memory_space=pl.ANY)] * 2,
        out_specs=[pl.BlockSpec(memory_space=pltpu.VMEM)] * late + [pl.BlockSpec(memory_space=pltpu.SMEM)],
        out_shape=[jax.ShapeDtypeStruct((2, KP, PIECE, BLOCK), BF16)] * late
        + [jax.ShapeDtypeStruct((2 * SLOTS + 1,), jnp.int32)],
        scratch_shapes=[pltpu.SemaphoreType.DMA((late, 2))],
        compiler_params=pltpu.CompilerParams(vmem_limit_bytes=60 << 20),
    )(table, left, right)
    return outs[:late], outs[late]


def product_kernel(*refs):
    moments, factors = refs[:8], refs[8:15]
    left, right = refs[15:17]
    outs = refs[17:25]
    left_all, right_all, moment_all, crossed, shaped, sem = refs[25:]
    group = lax.axis_index("group")

    @pl.when(has_slot(group))
    def _():
        slot = slot_at(group)
        copies = []
        for n, move in enumerate(MOVES):
            source = from_device(group, move)
            left_rows = left.at[slot] if n == 0 else factors[n - 1].at[0]
            right_rows = right.at[slot] if n == 0 else factors[n - 1].at[1]
            copies.append((
                pltpu.make_async_copy(left_rows, left_all.at[:, source], sem.at[0, n]),
                pltpu.make_async_copy(right_rows, right_all.at[:, source], sem.at[1, n]),
                pltpu.make_async_copy(moments[n], moment_all.at[:, source], sem.at[2, n]),
            ))
        for part in (0, 2, 1):
            for c in copies:
                c[part].start()
        for part in (0, 2):
            for c in copies:
                c[part].wait()
        moment = moment_all[...].reshape(BLOCK, BLOCK)
        step = 256
        for part in range(BLOCK // step):
            chunk = left_all[:, :, :, part * step : (part + 1) * step].reshape(BLOCK, step)
            crossed[part * step : (part + 1) * step, :] = lax.dot_general(
                chunk, moment, (((0,), (0,)), ((), ())), preferred_element_type=F32
            ).astype(BF16)
        for c in copies:
            c[1].wait()
        factor = right_all[...].reshape(BLOCK, BLOCK)
        total = jnp.zeros((1, BLOCK), F32)
        for part in range(BLOCK // step):
            value = jnp.dot(
                crossed[part * step : (part + 1) * step, :], factor, preferred_element_type=F32
            )
            shaped[part * step : (part + 1) * step, :] = value
            total += jnp.sum(value * value, axis=0, keepdims=True)
        shampoo_sq = jnp.sum(total, axis=1, keepdims=True)
        scale = 1.0 / jnp.sqrt(shampoo_sq + 1e-06)
        for n, move in enumerate(MOVES):
            dest = to_device(group, move)
            for k in range(KP):
                rows = pl.ds(pl.multiple_of(k * ROWS + dest * PIECE, PIECE), PIECE)
                outs[n][k] = (scale * shaped[rows, :]).astype(BF16)


def product(moments, factors, left, right):
    whole = pltpu.VMEM((KP, N_GROUP, PIECE, BLOCK), BF16)
    return pl.pallas_call(
        product_kernel,
        in_specs=[pl.BlockSpec(memory_space=pl.ANY)] * 17,
        out_specs=[pl.BlockSpec(memory_space=pltpu.VMEM)] * 8,
        out_shape=[jax.ShapeDtypeStruct((KP, PIECE, BLOCK), BF16)] * 8,
        scratch_shapes=[
            whole,
            whole,
            whole,
            pltpu.VMEM((BLOCK, BLOCK), BF16),
            pltpu.VMEM((BLOCK, BLOCK), F32),
            pltpu.SemaphoreType.DMA((3, 8)),
        ],
        compiler_params=pltpu.CompilerParams(vmem_limit_bytes=48 << 20),
    )(*moments, *factors, left, right)


def return_kernel(where, *refs):
    parts, out = refs[:8], refs[8]
    group = lax.axis_index("group")
    used = where[2 * SLOTS]
    for move, part in zip(MOVES, parts):
        source = from_device(group, move)
        slot = slot_at(source)

        @pl.when(has_slot(source) & (slot < used))
        def _():
            row_block = where[2 * slot]
            place = where[2 * slot + 1]
            lanes = pl.ds(pl.multiple_of(place * BLOCK, BLOCK), BLOCK)
            for k in range(KP):
                out[row_block * KP + k, :, lanes] = part[k]


def return_pack(parts, where):
    return pl.pallas_call(
        return_kernel,
        in_specs=[pl.BlockSpec(memory_space=pltpu.SMEM)] + [pl.BlockSpec(memory_space=pltpu.VMEM)] * 8,
        out_specs=pl.BlockSpec(memory_space=pltpu.VMEM),
        out_shape=jax.ShapeDtypeStruct((N_FSDP, PIECE, 2 * BLOCK), BF16),
        compiler_params=pltpu.CompilerParams(vmem_limit_bytes=32 << 20),
    )(where, *parts)


def place_kernel(table, sums, arrived, out, count):
    row_block = lax.axis_index("fsdp") // KP
    for i in range(N_FSDP):
        count[i] = 0
    root = jnp.sqrt(sums[...])
    for cb in range(NCB):
        owner = table[row_block * NCB + cb]
        place = count[owner]
        count[owner] = place + 1
        lanes = pl.ds(pl.multiple_of(place * BLOCK, BLOCK), BLOCK)
        rows = arrived[owner, :, lanes].astype(F32)
        out[:, cb * BLOCK : (cb + 1) * BLOCK] = (root[:1, cb : cb + 1] * rows).astype(BF16)


def place_rows(arrived, sums, table):
    return pl.pallas_call(
        place_kernel,
        in_specs=[pl.BlockSpec(memory_space=pltpu.SMEM)] + [pl.BlockSpec(memory_space=pltpu.VMEM)] * 2,
        out_specs=pl.BlockSpec(memory_space=pltpu.VMEM),
        out_shape=jax.ShapeDtypeStruct((PIECE, NCB * BLOCK), BF16),
        scratch_shapes=[pltpu.SMEM((N_FSDP,), jnp.int32)],
        compiler_params=pltpu.CompilerParams(vmem_limit_bytes=32 << 20),
    )(table, sums, arrived)


def move_in(rows, move):
    return lax.ppermute(rows, "group", pairs_in(move))


def move_out(rows, move):
    return lax.ppermute(rows, "group", pairs_out(move))


def add_from(sums, axis, bit):
    return sums + lax.ppermute(sums, axis, [(i, i ^ bit) for i in range(lax.axis_size(axis))])


def body(grad, momentum, second, left_root, right_root, owner_table):
    tie = lax.optimization_barrier
    left = left_root.reshape(SLOTS, KP, PIECE, BLOCK)
    right = right_root.reshape(SLOTS, KP, PIECE, BLOCK)
    packed, early = pack_rows(grad, momentum, left, right, owner_table)
    second, left, packed = tie((second, left, packed))
    arrived = lax.all_to_all(packed, "fsdp", split_axis=0, concat_axis=0, tiled=True)
    late, where = factor_rows(left, right, owner_table)
    factors = [move_in(r, m) for r, m in zip(list(early) + list(late), MOVES[1:])]
    new_momentum, new_second, sums = update_states(grad, momentum, second)
    arrived, waited, sums = tie((arrived, factors[:HELD], sums))
    factors = list(waited) + factors[HELD:]
    sent = collect(arrived, where)
    moments = [sent[0]] + [move_in(r, m) for r, m in zip(sent[1:], MOVES[1:])]
    moments, sums = tie((moments, add_from(sums, "fsdp", 1)))
    shaped = product(moments, factors, left, right)
    sums = add_from(sums, "fsdp", 2)
    parts = [shaped[0]] + [move_out(r, m) for r, m in zip(shaped[1:], MOVES[1:])]
    parts[1], sums = tie((parts[1], sums))
    sums = add_from(sums, "fsdp", 4)
    returning = return_pack(parts, where)
    returning, sums = tie((returning, sums))
    arriving = lax.all_to_all(returning, "fsdp", split_axis=0, concat_axis=0, tiled=True)
    for bit in (1, 2, 4):
        sums = add_from(sums, "group", bit)
    return place_rows(arriving, sums, owner_table), new_momentum, new_second


def solution(mesh):
    rows = P(("fsdp", "group"), None)
    factors = P("fsdp", None, "group", None, None)
    return jax.shard_map(
        body,
        mesh=mesh,
        in_specs=(rows, rows, rows, factors, factors, P()),
        out_specs=(rows, rows, rows),
        check_vma=False,
    )
```
